512 devices in a mesh: src: 16 (over y_lo, z), row: 32 (over x, y_hi, core).
Axes of the slice: x: 4, y: 8 (y_hi: 4, y_lo: 2; y = y_hi * 2 + y_lo), z: 8, core: 2. Of those that a mesh axis runs over, the one named last changes fastest.
Arguments:
- rhs_panels: bfloat16 [5, 2048, 2048], P(None, 'row', 'src'), may hold values from -6 to 6
- coupling: bfloat16 [10, 2048, 2048], P(None, 'row'), may hold values from -0.0625 to 0.0625
- block_inverse: bfloat16 [5, 2048, 2048], P(None, 'row'), as said below
- quadrupoles: int32 [16, 1024, 4], replicated, may hold values from 0 to 2047
- misfit: float32 [16, 1024], replicated, may hold values from -0.046875 to 0.046875
Outputs:
- potential: float32 [5, 2048, 2048], P(None, 'row', 'src')
- gradient: float32 [16, 5, 2048], P(None, None, ('row', 'src'))
The draws below stay inside these ranges and needn't reach their ends.
Inputs may be any that keep to these rules, and one draw needn't show every extreme that they name: Every block of block_inverse is symmetric positive definite.
All inputs are finite; a program needn't handle non-finite values.
Results may differ from the reference program's by a relative error of at most 0.025.
Values may be sent and summed in bfloat16 or wider, within the bound.
No kernel may reach another device: no remote copies, remote signals or barrier semaphores. Data moves between devices by JAX's collectives and lax.ppermute only.
A program may use at most 64 MiB of HBM per device.

```python
import jax
import jax.numpy as jnp
from jax import lax

NP = 5
P_SIZE = 2048
S = 2048
NF = 16
NM = 1024
NB = 10


def draw_block_inverse(key, part):
    base = jax.random.fold_in(key, 7)
    noise_key, diag_key = jax.random.split(base, 2)
    noise = jax.random.normal(noise_key, (NP, P_SIZE, P_SIZE), jnp.float32)
    symmetric = (noise + jnp.swapaxes(noise, 1, 2)) * (0.25 / (2.0 * P_SIZE) ** 0.5)
    scales = jax.random.uniform(diag_key, (NP, P_SIZE), jnp.float32, 0.8, 1.6)
    result = symmetric + jnp.eye(P_SIZE, dtype=jnp.float32)[None, :, :] * scales[:, :, None]
    return result.astype(jnp.bfloat16)


def with_ends(drawn, stream_key, least, largest):
    longest = drawn.shape.index(max(drawn.shape))
    spots = []
    for shift in (0, 1):
        where = [jax.random.randint(jax.random.fold_in(stream_key, axis), (), 0, length) for axis, length in enumerate(drawn.shape)]
        where[longest] = (where[longest] + shift) % drawn.shape[longest]
        spots.append(tuple(where))
    return drawn.at[spots[0]].set(least).at[spots[1]].set(largest)


def steps_of(key, dims, cuts, low, top_value):
    loudness, own = 1.0, jax.random.fold_in(key, 6)
    for axis_at, shards_of in cuts:
        steps = jnp.exp(jax.random.uniform(jax.random.fold_in(own, axis_at), (shards_of,), jnp.float32, low / len(cuts), top_value / len(cuts)))
        loudness = loudness * jnp.repeat(steps, dims[axis_at] // shards_of).reshape([-1 if axis == axis_at else 1 for axis in range(len(dims))])
    return loudness


def normal_values(key, shape, spread, reach, shards=(), held_as=jnp.bfloat16):
    gain = steps_of(key, shape, shards, -0.22, 0.18) if shards else 1.0
    array = jax.random.normal(key, shape, jnp.float32) * spread * gain
    return jnp.minimum(jnp.maximum(array, -reach), reach).astype(held_as)


def setup_inputs(seed: int = 0) -> dict:
    key_list = jax.random.split(jax.random.key(seed), 6)
    rhs_panels = normal_values(key_list[0], (NP, P_SIZE, S), 1.0, 6.0, ((1, 32), (2, 16)))
    coupling = normal_values(key_list[1], (NB, P_SIZE, P_SIZE), (4 * P_SIZE) ** -0.5, 0.0625, ((1, 32),))
    block_inverse = draw_block_inverse(jax.random.fold_in(key_list[5], 71), 0)
    quadrupoles = with_ends(jax.random.randint(key_list[3], (NF, NM, 4), 0, S), jax.random.fold_in(key_list[3], 1), 0, S - 1).astype(jnp.int32)
    misfit = normal_values(key_list[4], (NF, NM), (0.1 / NM ** 0.5), 0.046875, (), jnp.float32)
    return {"rhs_panels": rhs_panels, "coupling": coupling, "block_inverse": block_inverse, "quadrupoles": quadrupoles, "misfit": misfit}


def pair_index(later, earlier):
    return later * (later - 1) // 2 + earlier


def reference(rhs_panels, coupling, block_inverse, quadrupoles, misfit):
    forward = []
    for panel in range(NP):
        total = rhs_panels[panel].astype(jnp.float32)
        for earlier in range(panel):
            total = total - jnp.dot(coupling[pair_index(panel, earlier)], forward[earlier], preferred_element_type=jnp.float32)
        forward.append(total.astype(jnp.bfloat16))
    solved = [None] * NP
    rounded = [None] * NP
    for panel in reversed(range(NP)):
        total = jnp.dot(block_inverse[panel], forward[panel], preferred_element_type=jnp.float32)
        for later in range(panel + 1, NP):
            total = total - jnp.dot(coupling[pair_index(later, panel)].T, rounded[later], preferred_element_type=jnp.float32)
        solved[panel] = total
        rounded[panel] = total.astype(jnp.bfloat16)
    potential = jnp.stack(solved)
    flat = jnp.stack(rounded).reshape(NP * P_SIZE, S)

    def frame(items):
        picks, weights = items
        source_diff = flat[:, picks[:, 0]].astype(jnp.float32) - flat[:, picks[:, 1]].astype(jnp.float32)
        measure_diff = flat[:, picks[:, 2]].astype(jnp.float32) - flat[:, picks[:, 3]].astype(jnp.float32)
        return jnp.dot(source_diff * measure_diff, weights, precision=lax.Precision.HIGHEST)

    gradient = lax.map(frame, (quadrupoles, misfit)).reshape(NF, NP, P_SIZE)
    return potential, gradient
```

```python
import jax
import jax.numpy as jnp
from jax import lax
from jax.sharding import PartitionSpec as P

BF = jnp.bfloat16
F32 = jnp.float32


def pair_index(later, earlier):
    return later * (later - 1) // 2 + earlier


def dot(left, right, left_dim, right_dim):
    return lax.dot_general(
        left, right, (((left_dim,), (right_dim,)), ((), ())), preferred_element_type=F32
    )


def shards(rhs_panels, coupling, block_inverse, quadrupoles, misfit):
    panels, rows, width = rhs_panels.shape
    size = coupling.shape[2]
    chips = lax.axis_size("row") // 2
    half = width // 2
    core = lax.axis_index("row") % 2
    pairs = [(2 * p + c, 2 * p + 1 - c) for p in range(chips) for c in range(2)]
    same_core = [[2 * p + c for p in range(chips)] for c in range(2)]

    def swap(value):
        return lax.ppermute(value, "row", pairs)

    def in_order(mine, other, axis):
        return jnp.where(
            core == 0,
            jnp.concatenate([mine, other], axis=axis),
            jnp.concatenate([other, mine], axis=axis),
        )

    def exchange(blocks):
        return lax.all_to_all(
            blocks, "row", split_axis=0, concat_axis=0, tiled=True, axis_index_groups=same_core
        )

    def gather(value):
        got = exchange(jnp.broadcast_to(value[None], (chips,) + value.shape))
        return jnp.transpose(got, (1, 0, 2)).reshape(value.shape[0], size)

    flipped = jnp.transpose(rhs_panels, (0, 2, 1))
    keep = lax.dynamic_slice_in_dim(flipped, core * half, half, axis=1)
    send = lax.dynamic_slice_in_dim(flipped, (1 - core) * half, half, axis=1)
    rhs = in_order(keep, swap(send), 2)

    other_coupling = swap(coupling)
    other_inverse = swap(block_inverse)
    stacked = []
    for panel in range(panels):
        blocks = [
            in_order(coupling[i], other_coupling[i], 0)
            for i in (pair_index(later, panel) for later in range(panel + 1, panels))
        ]
        blocks.append(in_order(block_inverse[panel], other_inverse[panel], 0))
        stacked.append(jnp.concatenate(blocks, axis=0))

    tall = 2 * rows
    totals = [rhs[panel].astype(F32) for panel in range(panels)]
    for panel in range(panels):
        full = gather(totals[panel].astype(BF))
        out = dot(full, stacked[panel], 1, 1)
        for at, later in enumerate(range(panel + 1, panels)):
            totals[later] = totals[later] - out[:, at * tall : (at + 1) * tall]
        totals[panel] = out[:, (panels - 1 - panel) * tall :]

    solved = [None] * panels
    rounded = [None] * panels
    for panel in reversed(range(panels)):
        total = totals[panel]
        if panel < panels - 1:
            later = jnp.concatenate(rounded[panel + 1 :], axis=1)
            part = dot(later, stacked[panel][: later.shape[1]], 1, 0).astype(BF)
            part = jnp.transpose(part.reshape(half, chips, tall), (1, 0, 2))
            total = total - jnp.sum(exchange(part).astype(F32), axis=0)
        solved[panel] = total
        rounded[panel] = total.astype(BF)

    solved = jnp.stack(solved)
    keep = lax.dynamic_slice_in_dim(solved, core * rows, rows, axis=2)
    send = lax.dynamic_slice_in_dim(solved, (1 - core) * rows, rows, axis=2)
    potential = jnp.transpose(in_order(keep, swap(send), 1), (0, 2, 1))

    groups = lax.axis_size("src")
    nodes = potential.astype(BF).reshape(panels * rows, width)
    nodes = lax.all_to_all(
        jnp.broadcast_to(nodes[None], (groups,) + nodes.shape),
        "src",
        split_axis=0,
        concat_axis=0,
        tiled=True,
    )
    nodes = jnp.transpose(nodes, (1, 0, 2)).reshape(panels * rows, groups * width)
    frames, measures = misfit.shape
    share = frames // groups
    first = lax.axis_index("src") * share
    quads = lax.dynamic_slice_in_dim(quadrupoles, first, share, axis=0).reshape(share * measures, 4)
    weights = lax.dynamic_slice_in_dim(misfit, first, share, axis=0).reshape(1, share * measures)
    sources = lax.broadcasted_iota(jnp.int32, (groups * width, share * measures), 0)

    def difference(plus, minus):
        hot = (sources == quads[None, :, plus]).astype(BF)
        hot = hot - (sources == quads[None, :, minus]).astype(BF)
        return dot(nodes, hot, 1, 0)

    product = difference(0, 1) * difference(2, 3) * weights
    mine = jnp.sum(product.reshape(panels, groups, rows // groups, share, measures), axis=4)
    mine = jnp.transpose(mine, (1, 3, 0, 2))
    gradient = lax.all_to_all(mine, "src", split_axis=0, concat_axis=0, tiled=True)
    return (potential, gradient.reshape(frames, panels, rows // groups))


def solution(mesh):
    return jax.shard_map(
        shards,
        mesh=mesh,
        in_specs=(P(None, "row", "src"), P(None, "row", None), P(None, "row", None), P(), P()),
        out_specs=(P(None, "row", "src"), P(None, None, ("row", "src"))),
        check_vma=False,
    )
```

```python
import jax
import jax.numpy as jnp
from jax import lax
from jax.experimental import pallas as pl
from jax.sharding import PartitionSpec as P

BF = jnp.bfloat16
F32 = jnp.float32


def pair_index(later, earlier):
    return later * (later - 1) // 2 + earlier


def dot(left, right, left_dim, right_dim):
    return lax.dot_general(
        left, right, (((left_dim,), (right_dim,)), ((), ())), preferred_element_type=F32
    )


def weigh_kernel(table_ref, picks_ref, weights_ref, out_ref):
    parts, lines, depth = table_ref.shape
    frames, _, measures = picks_ref.shape
    table = table_ref[...].reshape(parts * lines, depth)
    span = min(256, measures)
    places = lax.broadcasted_iota(jnp.int32, (depth, span), 0)

    def frame(at, carry):
        total = jnp.zeros(out_ref.shape[1:], F32)
        for start in range(0, measures, span):
            values = []
            for which in range(4):
                index = picks_ref[at, which : which + 1, start : start + span]
                hot = jnp.where(places == index % depth, 1.0, 0.0).astype(BF)
                found = dot(table, hot, 1, 0)
                part = index // depth
                value = found[:lines]
                for other in range(1, parts):
                    piece = found[other * lines : (other + 1) * lines]
                    value = jnp.where(part == other, piece, value)
                values.append(value)
            product = (values[0] - values[1]) * (values[2] - values[3])
            product = product * weights_ref[pl.ds(at, 1), start : start + span]
            for lane in range(0, span, 128):
                total = total + product[:, lane : lane + 128]
        out_ref[at] = total
        return carry

    lax.fori_loop(0, frames, frame, 0)


def weigh(table, picks, weights):
    return pl.pallas_call(
        weigh_kernel,
        out_shape=jax.ShapeDtypeStruct((weights.shape[0], table.shape[1], 128), F32),
    )(table, picks, weights)


def shards(rhs_panels, coupling, block_inverse, quadrupoles, misfit):
    panels, rows, width = rhs_panels.shape
    size = coupling.shape[2]
    chips = lax.axis_size("row") // 2
    half = width // 2
    core = lax.axis_index("row") % 2
    pairs = [(2 * p + c, 2 * p + 1 - c) for p in range(chips) for c in range(2)]
    same_core = [[2 * p + c for p in range(chips)] for c in range(2)]

    def swap(value):
        return lax.ppermute(value, "row", pairs)

    def in_order(mine, other, axis):
        return jnp.where(
            core == 0,
            jnp.concatenate([mine, other], axis=axis),
            jnp.concatenate([other, mine], axis=axis),
        )

    def exchange(blocks):
        return lax.all_to_all(
            blocks, "row", split_axis=0, concat_axis=0, tiled=True, axis_index_groups=same_core
        )

    def gather(value):
        got = exchange(jnp.broadcast_to(value[None], (chips,) + value.shape))
        return jnp.transpose(got, (1, 0, 2)).reshape(value.shape[0], size)

    flipped = jnp.transpose(rhs_panels, (0, 2, 1))
    keep = lax.dynamic_slice_in_dim(flipped, core * half, half, axis=1)
    send = lax.dynamic_slice_in_dim(flipped, (1 - core) * half, half, axis=1)
    rhs = in_order(keep, swap(send), 2)
    rhs, coupling, block_inverse = lax.optimization_barrier((rhs, coupling, block_inverse))

    other_coupling = swap(coupling)
    other_inverse = swap(block_inverse)
    stacked = []
    for panel in range(panels):
        blocks = [
            in_order(coupling[i], other_coupling[i], 0)
            for i in (pair_index(later, panel) for later in range(panel + 1, panels))
        ]
        blocks.append(in_order(block_inverse[panel], other_inverse[panel], 0))
        stacked.append(jnp.concatenate(blocks, axis=0))

    tall = 2 * rows
    totals = [rhs[panel].astype(F32) for panel in range(panels)]
    for panel in range(panels):
        full = gather(totals[panel].astype(BF))
        out = dot(full, stacked[panel], 1, 1)
        for at, later in enumerate(range(panel + 1, panels)):
            totals[later] = totals[later] - out[:, at * tall : (at + 1) * tall]
        totals[panel] = out[:, (panels - 1 - panel) * tall :]

    groups = lax.axis_size("src")
    nodes = rows // groups

    def natural(value):
        keep = lax.dynamic_slice_in_dim(value, core * rows, rows, axis=1)
        send = lax.dynamic_slice_in_dim(value, (1 - core) * rows, rows, axis=1)
        return jnp.transpose(in_order(keep, swap(send), 0))

    rounded = [None] * panels
    potential = [None] * panels
    for panel in reversed(range(panels)):
        total = totals[panel]
        if panel < panels - 1:
            later = jnp.concatenate(rounded[panel + 1 :], axis=1)
            part = dot(later, stacked[panel][: later.shape[1]], 1, 0).astype(BF)
            part = jnp.transpose(part.reshape(half, chips, tall), (1, 0, 2))
            total = total - jnp.sum(exchange(part).astype(F32), axis=0)
        rounded[panel] = total.astype(BF)
        potential[panel] = natural(total)

    lines = panels * nodes
    table = jnp.stack([value.astype(BF).reshape(groups, nodes, width) for value in potential], 1)
    table = table.reshape(groups, lines, width)
    table = lax.all_to_all(table, "src", split_axis=0, concat_axis=0, tiled=True)
    table = jnp.transpose(table.reshape(groups // 2, 2, lines, width), (0, 2, 1, 3))
    table = table.reshape(groups // 2, lines, 2 * width)
    table = jnp.pad(table, ((0, 0), (0, -lines % 8), (0, 0)))
    sums = weigh(table, jnp.transpose(quadrupoles, (0, 2, 1)), misfit)
    gradient = jnp.sum(sums, axis=2)[:, :lines]
    return (jnp.stack(potential), gradient.reshape(misfit.shape[0], panels, nodes))


def solution(mesh):
    return jax.shard_map(
        shards,
        mesh=mesh,
        in_specs=(P(None, "row", "src"), P(None, "row", None), P(None, "row", None), P(), P()),
        out_specs=(P(None, "row", "src"), P(None, None, ("row", "src"))),
        check_vma=False,
    )
```

```python
import jax
import jax.numpy as jnp
from jax import lax
from jax.experimental import pallas as pl
from jax.sharding import PartitionSpec as P

BF = jnp.bfloat16
F32 = jnp.float32


def pair_index(later, earlier):
    return later * (later - 1) // 2 + earlier


def dot(left, right, left_dim, right_dim):
    return lax.dot_general(
        left, right, (((left_dim,), (right_dim,)), ((), ())), preferred_element_type=F32
    )


def weigh_kernel(table_ref, picks_ref, weights_ref, out_ref):
    groups, count, width = table_ref.shape
    panels, nodes, frames = out_ref.shape
    measures = picks_ref.shape[2]
    depth, parts = 2 * width, groups // 2
    lines = count + -count % 8
    table = []
    for part in range(parts):
        pair = [table_ref[2 * part].astype(F32), table_ref[2 * part + 1].astype(F32)]
        table.append(jnp.concatenate(pair, axis=1))
        table.append(jnp.zeros((lines - count, depth), F32))
    table = jnp.concatenate(table, axis=0).astype(BF)
    span = min(256, measures)
    places = lax.broadcasted_iota(jnp.int32, (depth, span), 0).astype(jnp.int16)
    lane = lax.broadcasted_iota(jnp.int32, (lines, 128), 1)

    def frame(at, result):
        total = jnp.zeros((lines, span), F32)
        for start in range(0, measures, span):
            values = []
            for which in range(4):
                index = picks_ref[at, which : which + 1, start : start + span]
                low = (index & (depth - 1)).astype(jnp.int16)
                hot = jnp.where(places == low, jnp.ones((), BF), jnp.zeros((), BF))
                found = dot(table, hot, 1, 0)
                part = index // depth
                value = found[:lines]
                for other in range(1, parts):
                    piece = found[other * lines : (other + 1) * lines]
                    value = jnp.where(part == other, piece, value)
                values.append(value)
            product = (values[0] - values[1]) * (values[2] - values[3])
            total = total + product * weights_ref[pl.ds(at, 1), start : start + span]
        return jnp.where(lane == at, jnp.sum(total, axis=1, keepdims=True), result)

    result = lax.fori_loop(0, frames, frame, jnp.zeros((lines, 128), F32), unroll=2)
    for panel in range(panels):
        out_ref[panel] = result[panel * nodes : (panel + 1) * nodes, :frames]


def weigh(table, picks, weights, panels):
    return pl.pallas_call(
        weigh_kernel,
        out_shape=jax.ShapeDtypeStruct(
            (panels, table.shape[1] // panels, weights.shape[0]), F32
        ),
    )(table, picks, weights)


def shards(rhs_panels, coupling, block_inverse, quadrupoles, misfit):
    panels, rows, width = rhs_panels.shape
    size = coupling.shape[2]
    chips = lax.axis_size("row") // 2
    half = width // 2
    core = lax.axis_index("row") % 2
    pairs = [(2 * p + c, 2 * p + 1 - c) for p in range(chips) for c in range(2)]
    same_core = [[2 * p + c for p in range(chips)] for c in range(2)]

    def swap(value):
        return lax.ppermute(value, "row", pairs)

    def in_order(mine, other, axis):
        return jnp.where(
            core == 0,
            jnp.concatenate([mine, other], axis=axis),
            jnp.concatenate([other, mine], axis=axis),
        )

    def exchange(blocks):
        return lax.all_to_all(
            blocks, "row", split_axis=0, concat_axis=0, tiled=True, axis_index_groups=same_core
        )

    def gather(value):
        got = exchange(jnp.broadcast_to(value[None], (chips,) + value.shape))
        return jnp.transpose(got, (1, 0, 2)).reshape(value.shape[0], size)

    def pieces_of(part):
        return jnp.transpose(part.astype(BF).reshape(half, chips, tall), (1, 0, 2))

    tall = 2 * rows
    groups = lax.axis_size("src")
    nodes = rows // groups

    flipped = jnp.transpose(rhs_panels, (0, 2, 1))
    keep = lax.dynamic_slice_in_dim(flipped, core * half, half, axis=1)
    send = lax.dynamic_slice_in_dim(flipped, (1 - core) * half, half, axis=1)
    rhs = in_order(keep, swap(send), 2)
    other_coupling = swap(coupling)
    other_inverse = swap(block_inverse)

    def factor(later, earlier):
        at = pair_index(later, earlier)
        return in_order(coupling[at], other_coupling[at], 0)

    factors = {
        (later, earlier): factor(later, earlier)
        for later in range(1, panels)
        for earlier in range(later)
    }
    inverses = [in_order(block_inverse[k], other_inverse[k], 0) for k in range(panels)]

    full = []
    for panel in range(panels):
        total = rhs[panel].astype(F32)
        for earlier in range(panel):
            total = total - dot(full[earlier], factors[panel, earlier], 1, 1)
        full.append(gather(total.astype(BF)))
    totals = [lax.optimization_barrier(dot(full[k], inverses[k], 1, 1)) for k in range(panels)]

    rounded = [None] * panels
    solved = [None] * panels
    for panel in reversed(range(panels)):
        total = totals[panel]
        if panel < panels - 1:
            part = dot(rounded[panels - 1], factors[panels - 1, panel], 1, 0)
            for later in reversed(range(panel + 1, panels - 1)):
                part = part + dot(rounded[later], factors[later, panel], 1, 0)
            total = total - jnp.sum(exchange(pieces_of(part)).astype(F32), axis=0)
        rounded[panel] = total.astype(BF)
        solved[panel] = total

    solved = jnp.stack(solved)
    keep = lax.dynamic_slice_in_dim(solved, core * rows, rows, axis=2)
    send = lax.dynamic_slice_in_dim(solved, (1 - core) * rows, rows, axis=2)
    potential = jnp.transpose(in_order(keep, swap(send), 1), (0, 2, 1))

    table = jnp.transpose(potential.astype(BF).reshape(panels, groups, nodes, width), (1, 0, 2, 3))
    table = table.reshape(groups, panels * nodes, width)
    table = lax.all_to_all(table, "src", split_axis=0, concat_axis=0, tiled=True)
    sums = weigh(table, jnp.transpose(quadrupoles, (0, 2, 1)), misfit, panels)
    gradient = jnp.transpose(sums, (2, 0, 1))
    return (potential, gradient)


def solution(mesh):
    return jax.shard_map(
        shards,
        mesh=mesh,
        in_specs=(P(None, "row", "src"), P(None, "row", None), P(None, "row", None), P(), P()),
        out_specs=(P(None, "row", "src"), P(None, None, ("row", "src"))),
        check_vma=False,
    )
```

```python
import jax
import jax.numpy as jnp
from jax import lax
from jax.experimental import pallas as pl
from jax.experimental.pallas import tpu as pltpu
from jax.sharding import PartitionSpec as P

BF = jnp.bfloat16
F32 = jnp.float32


def pair_index(later, earlier):
    return later * (later - 1) // 2 + earlier


def dot(left, right, left_dim, right_dim):
    return lax.dot_general(
        left, right, (((left_dim,), (right_dim,)), ((), ())), preferred_element_type=F32
    )


SCALAR = pl.BlockSpec(memory_space=pltpu.SMEM)
WHOLE = pl.BlockSpec(memory_space=pltpu.VMEM)
PARAMS = pltpu.CompilerParams(vmem_limit_bytes=24 * 1024 * 1024)


def lay_rows(core, mine_ref, other_ref, wide_ref):
    rows = mine_ref.shape[0]
    wide_ref[pl.ds(pl.multiple_of(core * rows, rows), rows)] = mine_ref[...]
    wide_ref[pl.ds(pl.multiple_of((1 - core) * rows, rows), rows)] = other_ref[...]


def lay_columns(got_ref, full_ref):
    for chip in range(got_ref.shape[0]):
        lanes = got_ref.shape[2]
        full_ref[:, chip * lanes : (chip + 1) * lanes] = got_ref[chip]


def ahead_kernel(core_ref, base_ref, got_ref, mine_ref, other_ref, out_ref, wide_ref, full_ref):
    lay_rows(core_ref[0], mine_ref, other_ref, wide_ref)
    lay_columns(got_ref, full_ref)
    value = base_ref[...] - dot(full_ref[...], wide_ref[...], 1, 1)
    value = value.astype(BF)
    for chip in range(out_ref.shape[0]):
        out_ref[chip] = value


def send_pieces(part, out_ref):
    lanes = out_ref.shape[2]
    for chip in range(out_ref.shape[0]):
        out_ref[chip] = part[:, chip * lanes : (chip + 1) * lanes].astype(BF)


def turn_kernel(
    core_ref, got_ref, mine_d_ref, other_d_ref, mine_ref, other_ref, out_ref, x_ref, wide_ref, full_ref
):
    lay_rows(core_ref[0], mine_d_ref, other_d_ref, wide_ref)
    lay_columns(got_ref, full_ref)
    value = dot(full_ref[...], wide_ref[...], 1, 1)
    x_ref[...] = value
    lay_rows(core_ref[0], mine_ref, other_ref, wide_ref)
    send_pieces(dot(value.astype(BF), wide_ref[...], 1, 0), out_ref)


def back_kernel(
    core_ref, base_ref, got_ref, part_ref, mine_ref, other_ref, out_ref, x_ref, wide_ref
):
    lay_rows(core_ref[0], mine_ref, other_ref, wide_ref)
    value = base_ref[...]
    for chip in range(got_ref.shape[0]):
        value = value - got_ref[chip].astype(F32)
    x_ref[...] = value
    part = part_ref[...] + dot(value.astype(BF), wide_ref[...], 1, 0)
    send_pieces(part, out_ref)


def call(kernel, core, operands, got, solved, full):
    size = got.shape[0] * got.shape[2]
    out = jax.ShapeDtypeStruct(got.shape, BF)
    x = jax.ShapeDtypeStruct(got.shape[1:], F32)
    scratch = [pltpu.VMEM((got.shape[2], size), BF)]
    if full:
        scratch.append(pltpu.VMEM((got.shape[1], size), BF))
    return pl.pallas_call(
        kernel,
        out_shape=(out, x) if solved else out,
        in_specs=[SCALAR] + [WHOLE] * len(operands),
        out_specs=(WHOLE, WHOLE) if solved else WHOLE,
        scratch_shapes=scratch,
        compiler_params=PARAMS,
    )(core, *operands)


def weigh_kernel(table_ref, picks_ref, weights_ref, out_ref):
    groups, count, width = table_ref.shape
    panels, nodes, frames = out_ref.shape
    measures = picks_ref.shape[2]
    depth, parts = 2 * width, groups // 2
    lines = count + -count % 8
    table = []
    for part in range(parts):
        pair = [table_ref[2 * part].astype(F32), table_ref[2 * part + 1].astype(F32)]
        table.append(jnp.concatenate(pair, axis=1))
        table.append(jnp.zeros((lines - count, depth), F32))
    table = jnp.concatenate(table, axis=0).astype(BF)
    span = min(256, measures)
    places = lax.broadcasted_iota(jnp.int32, (depth, span), 0).astype(jnp.int16)
    lane = lax.broadcasted_iota(jnp.int32, (lines, 128), 1)

    def frame(at, result):
        total = jnp.zeros((lines, span), F32)
        for start in range(0, measures, span):
            values = []
            for which in range(4):
                index = picks_ref[at, which : which + 1, start : start + span]
                low = (index & (depth - 1)).astype(jnp.int16)
                hot = jnp.where(places == low, jnp.ones((), BF), jnp.zeros((), BF))
                found = dot(table, hot, 1, 0)
                part = index // depth
                value = found[:lines]
                for other in range(1, parts):
                    piece = found[other * lines : (other + 1) * lines]
                    value = jnp.where(part == other, piece, value)
                values.append(value)
            product = (values[0] - values[1]) * (values[2] - values[3])
            total = total + product * weights_ref[pl.ds(at, 1), start : start + span]
        return jnp.where(lane == at, jnp.sum(total, axis=1, keepdims=True), result)

    result = lax.fori_loop(0, frames, frame, jnp.zeros((lines, 128), F32), unroll=2)
    for panel in range(panels):
        out_ref[panel] = result[panel * nodes : (panel + 1) * nodes, :frames]


def weigh(table, picks, weights, panels):
    return pl.pallas_call(
        weigh_kernel,
        out_shape=jax.ShapeDtypeStruct(
            (panels, table.shape[1] // panels, weights.shape[0]), F32
        ),
        in_specs=[WHOLE] * 3,
        out_specs=WHOLE,
        compiler_params=PARAMS,
    )(table, picks, weights)


def shards(rhs_panels, coupling, block_inverse, quadrupoles, misfit):
    panels, rows, width = rhs_panels.shape
    size = coupling.shape[2]
    chips = lax.axis_size("row") // 2
    half = width // 2
    core = lax.axis_index("row") % 2
    pairs = [(2 * p + c, 2 * p + 1 - c) for p in range(chips) for c in range(2)]
    same_core = [[2 * p + c for p in range(chips)] for c in range(2)]

    def swap(value):
        return lax.ppermute(value, "row", pairs)

    def in_order(mine, other, axis):
        return jnp.where(
            core == 0,
            jnp.concatenate([mine, other], axis=axis),
            jnp.concatenate([other, mine], axis=axis),
        )

    def exchange(blocks):
        return lax.all_to_all(
            blocks, "row", split_axis=0, concat_axis=0, tiled=True, axis_index_groups=same_core
        )

    def collect(got):
        return jnp.transpose(got, (1, 0, 2)).reshape(half, size)

    tall = 2 * rows
    groups = lax.axis_size("src")
    nodes = rows // groups

    flipped = jnp.transpose(rhs_panels, (0, 2, 1))
    keep = lax.dynamic_slice_in_dim(flipped, core * half, half, axis=1)
    send = lax.dynamic_slice_in_dim(flipped, (1 - core) * half, half, axis=1)
    rhs = in_order(keep, swap(send), 2)
    other_coupling = swap(coupling)
    other_inverse = swap(block_inverse)

    def factor(later, earlier):
        at = pair_index(later, earlier)
        return in_order(coupling[at], other_coupling[at], 0)

    factors = {
        (later, earlier): factor(later, earlier)
        for later in range(1, panels)
        for earlier in range(later)
    }
    inverses = [in_order(block_inverse[k], other_inverse[k], 0) for k in range(panels)]

    def halves(later, earlier):
        at = pair_index(later, earlier)
        return [coupling[at], other_coupling[at]]

    place = core.reshape(1)
    message = jnp.broadcast_to(rhs[0][None], (chips,) + rhs[0].shape)
    full = []
    for panel in range(panels):
        got = exchange(message)
        full.append(collect(got))
        if panel + 1 < panels:
            base = rhs[panel + 1].astype(F32)
            for earlier in range(panel):
                base = base - dot(full[earlier], factors[panel + 1, earlier], 1, 1)
            operands = [base, got] + halves(panel + 1, panel)
            message = call(ahead_kernel, place, operands, got, False, True)
    totals = [
        lax.optimization_barrier(dot(full[k], inverses[k], 1, 1)) for k in range(panels - 1)
    ]

    last = panels - 1
    solved = [None] * panels
    rounded = [None] * panels
    operands = [got, block_inverse[last], other_inverse[last]] + halves(last, last - 1)
    message, solved[last] = call(turn_kernel, place, operands, got, True, True)
    for panel in reversed(range(last)):
        rounded[panel + 1] = solved[panel + 1].astype(BF)
        got = exchange(message)
        if panel:
            part = dot(rounded[last], factors[last, panel - 1], 1, 0)
            for later in reversed(range(panel + 1, last)):
                part = part + dot(rounded[later], factors[later, panel - 1], 1, 0)
            operands = [totals[panel], got, part] + halves(panel, panel - 1)
            message, solved[panel] = call(back_kernel, place, operands, got, True, False)
        else:
            solved[panel] = totals[panel] - jnp.sum(got.astype(F32), axis=0)

    solved = jnp.stack(solved)
    keep = lax.dynamic_slice_in_dim(solved, core * rows, rows, axis=2)
    send = lax.dynamic_slice_in_dim(solved, (1 - core) * rows, rows, axis=2)
    potential = jnp.transpose(in_order(keep, swap(send), 1), (0, 2, 1))

    table = jnp.transpose(potential.astype(BF).reshape(panels, groups, nodes, width), (1, 0, 2, 3))
    table = table.reshape(groups, panels * nodes, width)
    table = lax.all_to_all(table, "src", split_axis=0, concat_axis=0, tiled=True)
    sums = weigh(table, jnp.transpose(quadrupoles, (0, 2, 1)), misfit, panels)
    gradient = jnp.transpose(sums, (2, 0, 1))
    return (potential, gradient)


def solution(mesh):
    return jax.shard_map(
        shards,
        mesh=mesh,
        in_specs=(P(None, "row", "src"), P(None, "row", None), P(None, "row", None), P(), P()),
        out_specs=(P(None, "row", "src"), P(None, None, ("row", "src"))),
        check_vma=False,
    )
```

```python
import jax
import jax.numpy as jnp
from jax import lax
from jax.experimental import pallas as pl
from jax.experimental.pallas import tpu as pltpu
from jax.sharding import PartitionSpec as P

BF = jnp.bfloat16
F32 = jnp.float32


def pair_index(later, earlier):
    return later * (later - 1) // 2 + earlier


def dot(left, right, left_dim, right_dim):
    return lax.dot_general(
        left, right, (((left_dim,), (right_dim,)), ((), ())), preferred_element_type=F32
    )


SCALAR = pl.BlockSpec(memory_space=pltpu.SMEM)
WHOLE = pl.BlockSpec(memory_space=pltpu.VMEM)
PARAMS = pltpu.CompilerParams(vmem_limit_bytes=24 * 1024 * 1024)


def lay_rows(core, mine_ref, other_ref, wide_ref):
    rows = mine_ref.shape[0]
    wide_ref[pl.ds(pl.multiple_of(core * rows, rows), rows)] = mine_ref[...]
    wide_ref[pl.ds(pl.multiple_of((1 - core) * rows, rows), rows)] = other_ref[...]


def lay_columns(got_ref, full_ref):
    for chip in range(got_ref.shape[0]):
        lanes = got_ref.shape[2]
        full_ref[:, chip * lanes : (chip + 1) * lanes] = got_ref[chip]


def ahead_kernel(core_ref, base_ref, got_ref, mine_ref, other_ref, out_ref, wide_ref, full_ref):
    lay_rows(core_ref[0], mine_ref, other_ref, wide_ref)
    lay_columns(got_ref, full_ref)
    value = base_ref[...] - dot(full_ref[...], wide_ref[...], 1, 1)
    value = value.astype(BF)
    for chip in range(out_ref.shape[0]):
        out_ref[chip] = value


def send_pieces(part, out_ref):
    lanes = out_ref.shape[2]
    for chip in range(out_ref.shape[0]):
        out_ref[chip] = part[:, chip * lanes : (chip + 1) * lanes].astype(BF)


def turn_kernel(
    core_ref, got_ref, mine_d_ref, other_d_ref, mine_ref, other_ref, out_ref, x_ref, wide_ref, full_ref
):
    lay_rows(core_ref[0], mine_d_ref, other_d_ref, wide_ref)
    lay_columns(got_ref, full_ref)
    value = dot(full_ref[...], wide_ref[...], 1, 1)
    x_ref[...] = value
    lay_rows(core_ref[0], mine_ref, other_ref, wide_ref)
    send_pieces(dot(value.astype(BF), wide_ref[...], 1, 0), out_ref)


def back_kernel(
    core_ref, base_ref, got_ref, part_ref, mine_ref, other_ref, out_ref, x_ref, wide_ref
):
    lay_rows(core_ref[0], mine_ref, other_ref, wide_ref)
    value = base_ref[...]
    for chip in range(got_ref.shape[0]):
        value = value - got_ref[chip].astype(F32)
    x_ref[...] = value
    part = part_ref[...] + dot(value.astype(BF), wide_ref[...], 1, 0)
    send_pieces(part, out_ref)


def call(kernel, core, operands, got, solved, full):
    size = got.shape[0] * got.shape[2]
    out = jax.ShapeDtypeStruct(got.shape, BF)
    x = jax.ShapeDtypeStruct(got.shape[1:], F32)
    scratch = [pltpu.VMEM((got.shape[2], size), BF)]
    if full:
        scratch.append(pltpu.VMEM((got.shape[1], size), BF))
    return pl.pallas_call(
        kernel,
        out_shape=(out, x) if solved else out,
        in_specs=[SCALAR] + [WHOLE] * len(operands),
        out_specs=(WHOLE, WHOLE) if solved else WHOLE,
        scratch_shapes=scratch,
        compiler_params=PARAMS,
    )(core, *operands)


def weigh_kernel(table_ref, picks_ref, weights_ref, out_ref):
    groups, count, width = table_ref.shape
    panels, nodes, frames = out_ref.shape
    measures = picks_ref.shape[2]
    depth, parts = 2 * width, groups // 2
    lines = count + -count % 8
    table = []
    for part in range(parts):
        pair = [table_ref[2 * part].astype(F32), table_ref[2 * part + 1].astype(F32)]
        table.append(jnp.concatenate(pair, axis=1))
        table.append(jnp.zeros((lines - count, depth), F32))
    table = jnp.concatenate(table, axis=0).astype(BF)
    span = min(256, measures)
    places = lax.broadcasted_iota(jnp.int32, (depth, span), 0).astype(jnp.int16)
    lane = lax.broadcasted_iota(jnp.int32, (lines, 128), 1)

    def frame(at, result):
        total = jnp.zeros((lines, span), F32)
        for start in range(0, measures, span):
            values = []
            for which in range(4):
                index = picks_ref[at, which : which + 1, start : start + span]
                low = (index & (depth - 1)).astype(jnp.int16)
                hot = jnp.where(places == low, jnp.ones((), BF), jnp.zeros((), BF))
                found = dot(table, hot, 1, 0)
                part = index // depth
                value = found[:lines]
                for other in range(1, parts):
                    piece = found[other * lines : (other + 1) * lines]
                    value = jnp.where(part == other, piece, value)
                values.append(value)
            product = (values[0] - values[1]) * (values[2] - values[3])
            total = total + product * weights_ref[pl.ds(at, 1), start : start + span]
        return jnp.where(lane == at, jnp.sum(total, axis=1, keepdims=True), result)

    result = lax.fori_loop(0, frames, frame, jnp.zeros((lines, 128), F32), unroll=8)
    for panel in range(panels):
        out_ref[panel] = result[panel * nodes : (panel + 1) * nodes, :frames]


def weigh(table, picks, weights, panels):
    return pl.pallas_call(
        weigh_kernel,
        out_shape=jax.ShapeDtypeStruct(
            (panels, table.shape[1] // panels, weights.shape[0]), F32
        ),
        in_specs=[WHOLE] * 3,
        out_specs=WHOLE,
        compiler_params=PARAMS,
    )(table, picks, weights)


def shards(rhs_panels, coupling, block_inverse, quadrupoles, misfit):
    panels, rows, width = rhs_panels.shape
    size = coupling.shape[2]
    chips = lax.axis_size("row") // 2
    half = width // 2
    core = lax.axis_index("row") % 2
    pairs = [(2 * p + c, 2 * p + 1 - c) for p in range(chips) for c in range(2)]
    same_core = [[2 * p + c for p in range(chips)] for c in range(2)]

    def swap(value):
        return lax.ppermute(value, "row", pairs)

    def in_order(mine, other, axis):
        return jnp.where(
            core == 0,
            jnp.concatenate([mine, other], axis=axis),
            jnp.concatenate([other, mine], axis=axis),
        )

    def exchange(blocks):
        return lax.all_to_all(
            blocks, "row", split_axis=0, concat_axis=0, tiled=True, axis_index_groups=same_core
        )

    def collect(got):
        return jnp.transpose(got, (1, 0, 2)).reshape(half, size)

    tall = 2 * rows
    groups = lax.axis_size("src")
    nodes = rows // groups

    flipped = jnp.transpose(rhs_panels, (0, 2, 1))
    keep = lax.dynamic_slice_in_dim(flipped, core * half, half, axis=1)
    send = lax.dynamic_slice_in_dim(flipped, (1 - core) * half, half, axis=1)
    rhs = in_order(keep, swap(send), 2)
    other_coupling = swap(coupling)
    other_inverse = swap(block_inverse)

    message = jnp.broadcast_to(rhs[0][None], (chips,) + rhs[0].shape)
    message, coupling = lax.optimization_barrier((message, coupling))

    def factor(later, earlier):
        at = pair_index(later, earlier)
        return in_order(coupling[at], other_coupling[at], 0)

    factors = {
        (later, earlier): factor(later, earlier)
        for later in range(1, panels)
        for earlier in range(later)
    }
    inverses = [in_order(block_inverse[k], other_inverse[k], 0) for k in range(panels)]

    def halves(later, earlier):
        at = pair_index(later, earlier)
        return [coupling[at], other_coupling[at]]

    place = core.reshape(1)
    full = []
    for panel in range(panels):
        got = exchange(message)
        full.append(collect(got))
        if panel + 1 < panels:
            base = rhs[panel + 1].astype(F32)
            for earlier in range(panel):
                base = base - dot(full[earlier], factors[panel + 1, earlier], 1, 1)
            operands = [base, got] + halves(panel + 1, panel)
            message = call(ahead_kernel, place, operands, got, False, True)
    totals = [
        lax.optimization_barrier(dot(full[k], inverses[k], 1, 1)) for k in range(panels - 1)
    ]

    last = panels - 1
    solved = [None] * panels
    rounded = [None] * panels
    operands = [got, block_inverse[last], other_inverse[last]] + halves(last, last - 1)
    message, solved[last] = call(turn_kernel, place, operands, got, True, True)
    for panel in reversed(range(last)):
        rounded[panel + 1] = solved[panel + 1].astype(BF)
        got = exchange(message)
        if panel:
            part = dot(rounded[last], factors[last, panel - 1], 1, 0)
            for later in reversed(range(panel + 1, last)):
                part = part + dot(rounded[later], factors[later, panel - 1], 1, 0)
            operands = [totals[panel], got, part] + halves(panel, panel - 1)
            message, solved[panel] = call(back_kernel, place, operands, got, True, False)
        else:
            solved[panel] = totals[panel] - jnp.sum(got.astype(F32), axis=0)

    solved = jnp.stack(solved)
    keep = lax.dynamic_slice_in_dim(solved, core * rows, rows, axis=2)
    send = lax.dynamic_slice_in_dim(solved, (1 - core) * rows, rows, axis=2)
    potential = jnp.transpose(in_order(keep, swap(send), 1), (0, 2, 1))

    table = jnp.transpose(potential.astype(BF).reshape(panels, groups, nodes, width), (1, 0, 2, 3))
    table = table.reshape(groups, panels * nodes, width)
    table = lax.all_to_all(table, "src", split_axis=0, concat_axis=0, tiled=True)
    sums = weigh(table, jnp.transpose(quadrupoles, (0, 2, 1)), misfit, panels)
    gradient = jnp.transpose(sums, (2, 0, 1))
    return (potential, gradient)


def solution(mesh):
    return jax.shard_map(
        shards,
        mesh=mesh,
        in_specs=(P(None, "row", "src"), P(None, "row", None), P(None, "row", None), P(), P()),
        out_specs=(P(None, "row", "src"), P(None, None, ("row", "src"))),
        check_vma=False,
    )
```

```python
import jax
import jax.numpy as jnp
from jax import lax
from jax.experimental import pallas as pl
from jax.experimental.pallas import tpu as pltpu
from jax.sharding import PartitionSpec as P

BF = jnp.bfloat16
F32 = jnp.float32


def pair_index(later, earlier):
    return later * (later - 1) // 2 + earlier


def dot(left, right, left_dim, right_dim):
    return lax.dot_general(
        left, right, (((left_dim,), (right_dim,)), ((), ())), preferred_element_type=F32
    )


SCALAR = pl.BlockSpec(memory_space=pltpu.SMEM)
WHOLE = pl.BlockSpec(memory_space=pltpu.VMEM)
PARAMS = pltpu.CompilerParams(vmem_limit_bytes=24 * 1024 * 1024)


def lay_rows(core, mine_ref, other_ref, wide_ref):
    rows = mine_ref.shape[0]
    wide_ref[pl.ds(pl.multiple_of(core * rows, rows), rows)] = mine_ref[...]
    wide_ref[pl.ds(pl.multiple_of((1 - core) * rows, rows), rows)] = other_ref[...]


def lay_columns(got_ref, full_ref):
    for chip in range(got_ref.shape[0]):
        lanes = got_ref.shape[2]
        full_ref[:, chip * lanes : (chip + 1) * lanes] = got_ref[chip]


def ahead_kernel(core_ref, base_ref, got_ref, mine_ref, other_ref, out_ref, wide_ref, full_ref):
    lay_rows(core_ref[0], mine_ref, other_ref, wide_ref)
    lay_columns(got_ref, full_ref)
    value = base_ref[...] - dot(full_ref[...], wide_ref[...], 1, 1)
    value = value.astype(BF)
    for chip in range(out_ref.shape[0]):
        out_ref[chip] = value


def send_pieces(part, out_ref):
    lanes = out_ref.shape[2]
    for chip in range(out_ref.shape[0]):
        out_ref[chip] = part[:, chip * lanes : (chip + 1) * lanes].astype(BF)


def turn_kernel(
    core_ref, got_ref, mine_d_ref, other_d_ref, mine_ref, other_ref, out_ref, x_ref, wide_ref, full_ref
):
    lay_rows(core_ref[0], mine_d_ref, other_d_ref, wide_ref)
    lay_columns(got_ref, full_ref)
    value = dot(full_ref[...], wide_ref[...], 1, 1)
    x_ref[...] = value
    lay_rows(core_ref[0], mine_ref, other_ref, wide_ref)
    send_pieces(dot(value.astype(BF), wide_ref[...], 1, 0), out_ref)


def back_kernel(
    core_ref, base_ref, got_ref, part_ref, mine_ref, other_ref, out_ref, x_ref, wide_ref
):
    lay_rows(core_ref[0], mine_ref, other_ref, wide_ref)
    value = base_ref[...]
    for chip in range(got_ref.shape[0]):
        value = value - got_ref[chip].astype(F32)
    x_ref[...] = value
    part = part_ref[...] + dot(value.astype(BF), wide_ref[...], 1, 0)
    send_pieces(part, out_ref)


def call(kernel, core, operands, got, solved, full):
    size = got.shape[0] * got.shape[2]
    out = jax.ShapeDtypeStruct(got.shape, BF)
    x = jax.ShapeDtypeStruct(got.shape[1:], F32)
    scratch = [pltpu.VMEM((got.shape[2], size), BF)]
    if full:
        scratch.append(pltpu.VMEM((got.shape[1], size), BF))
    return pl.pallas_call(
        kernel,
        out_shape=(out, x) if solved else out,
        in_specs=[SCALAR] + [WHOLE] * len(operands),
        out_specs=(WHOLE, WHOLE) if solved else WHOLE,
        scratch_shapes=scratch,
        compiler_params=PARAMS,
    )(core, *operands)


def weigh_kernel(table_ref, picks_ref, weights_ref, out_ref):
    groups, count, width = table_ref.shape
    panels, nodes, frames = out_ref.shape
    measures = picks_ref.shape[2]
    depth, parts = 2 * width, groups // 2
    lines = count + -count % 8
    table = []
    for part in range(parts):
        pair = [table_ref[2 * part].astype(F32), table_ref[2 * part + 1].astype(F32)]
        table.append(jnp.concatenate(pair, axis=1))
        table.append(jnp.zeros((lines - count, depth), F32))
    table = jnp.concatenate(table, axis=0).astype(BF)
    span = min(256, measures)
    places = lax.broadcasted_iota(jnp.int32, (depth, span), 0).astype(jnp.int16)
    lane = lax.broadcasted_iota(jnp.int32, (lines, 128), 1)

    def frame(at, result):
        total = jnp.zeros((lines, span), F32)
        for start in range(0, measures, span):
            values = []
            for which in range(4):
                index = picks_ref[at, which : which + 1, start : start + span]
                low = (index & (depth - 1)).astype(jnp.int16)
                hot = jnp.where(places == low, jnp.ones((), BF), jnp.zeros((), BF))
                found = dot(table, hot, 1, 0)
                part = index >> (depth.bit_length() - 1)
                value = found[:lines]
                for other in range(1, parts):
                    piece = found[other * lines : (other + 1) * lines]
                    value = jnp.where(part == other, piece, value)
                values.append(value)
            product = (values[0] - values[1]) * (values[2] - values[3])
            total = total + product * weights_ref[pl.ds(at, 1), start : start + span]
        return jnp.where(lane == at, jnp.sum(total, axis=1, keepdims=True), result)

    result = lax.fori_loop(0, frames, frame, jnp.zeros((lines, 128), F32), unroll=8)
    for panel in range(panels):
        out_ref[panel] = result[panel * nodes : (panel + 1) * nodes, :frames]


def weigh(table, picks, weights, panels):
    return pl.pallas_call(
        weigh_kernel,
        out_shape=jax.ShapeDtypeStruct(
            (panels, table.shape[1] // panels, weights.shape[0]), F32
        ),
        in_specs=[WHOLE] * 3,
        out_specs=WHOLE,
        compiler_params=PARAMS,
    )(table, picks, weights)


def shards(rhs_panels, coupling, block_inverse, quadrupoles, misfit):
    panels, rows, width = rhs_panels.shape
    size = coupling.shape[2]
    chips = lax.axis_size("row") // 2
    half = width // 2
    core = lax.axis_index("row") % 2
    pairs = [(2 * p + c, 2 * p + 1 - c) for p in range(chips) for c in range(2)]
    same_core = [[2 * p + c for p in range(chips)] for c in range(2)]

    def swap(value):
        return lax.ppermute(value, "row", pairs)

    def in_order(mine, other, axis):
        return jnp.where(
            core == 0,
            jnp.concatenate([mine, other], axis=axis),
            jnp.concatenate([other, mine], axis=axis),
        )

    def exchange(blocks):
        return lax.all_to_all(
            blocks, "row", split_axis=0, concat_axis=0, tiled=True, axis_index_groups=same_core
        )

    def collect(got):
        return jnp.transpose(got, (1, 0, 2)).reshape(half, size)

    tall = 2 * rows
    groups = lax.axis_size("src")
    nodes = rows // groups

    flipped = jnp.transpose(rhs_panels, (0, 2, 1))
    keep = lax.dynamic_slice_in_dim(flipped, core * half, half, axis=1)
    send = lax.dynamic_slice_in_dim(flipped, (1 - core) * half, half, axis=1)
    rhs = in_order(keep, swap(send), 2)
    other_coupling = swap(coupling)
    other_inverse = swap(block_inverse)

    message = jnp.broadcast_to(rhs[0][None], (chips,) + rhs[0].shape)
    message, coupling = lax.optimization_barrier((message, coupling))

    def factor(later, earlier):
        at = pair_index(later, earlier)
        return in_order(coupling[at], other_coupling[at], 0)

    factors = {
        (later, earlier): factor(later, earlier)
        for later in range(1, panels)
        for earlier in range(later)
    }
    inverses = [in_order(block_inverse[k], other_inverse[k], 0) for k in range(panels)]

    def halves(later, earlier):
        at = pair_index(later, earlier)
        return [coupling[at], other_coupling[at]]

    place = core.reshape(1)
    full = []
    for panel in range(panels):
        got = exchange(message)
        full.append(collect(got))
        if panel + 1 < panels:
            base = rhs[panel + 1].astype(F32)
            for earlier in range(panel):
                base = base - dot(full[earlier], factors[panel + 1, earlier], 1, 1)
            operands = [base, got] + halves(panel + 1, panel)
            message = call(ahead_kernel, place, operands, got, False, True)
    totals = [
        lax.optimization_barrier(dot(full[k], inverses[k], 1, 1)) for k in range(panels - 1)
    ]

    last = panels - 1
    solved = [None] * panels
    rounded = [None] * panels
    operands = [got, block_inverse[last], other_inverse[last]] + halves(last, last - 1)
    message, solved[last] = call(turn_kernel, place, operands, got, True, True)
    for panel in reversed(range(last)):
        rounded[panel + 1] = solved[panel + 1].astype(BF)
        if panel == 0:
            message, totals[0] = lax.optimization_barrier((message, totals[0]))
        got = exchange(message)
        if panel:
            part = dot(rounded[last], factors[last, panel - 1], 1, 0)
            for later in reversed(range(panel + 1, last)):
                part = part + dot(rounded[later], factors[later, panel - 1], 1, 0)
            operands = [totals[panel], got, part] + halves(panel, panel - 1)
            message, solved[panel] = call(back_kernel, place, operands, got, True, False)
        else:
            solved[panel] = totals[panel] - jnp.sum(got.astype(F32), axis=0)

    solved = jnp.stack(solved)
    keep = lax.dynamic_slice_in_dim(solved, core * rows, rows, axis=2)
    send = lax.dynamic_slice_in_dim(solved, (1 - core) * rows, rows, axis=2)
    potential = jnp.transpose(in_order(keep, swap(send), 1), (0, 2, 1))

    table = jnp.transpose(potential.astype(BF).reshape(panels, groups, nodes, width), (1, 0, 2, 3))
    table = table.reshape(groups, panels * nodes, width)
    table = lax.all_to_all(table, "src", split_axis=0, concat_axis=0, tiled=True)
    sums = weigh(table, jnp.transpose(quadrupoles, (0, 2, 1)), misfit, panels)
    gradient = jnp.transpose(sums, (2, 0, 1))
    return (potential, gradient)


def solution(mesh):
    return jax.shard_map(
        shards,
        mesh=mesh,
        in_specs=(P(None, "row", "src"), P(None, "row", None), P(None, "row", None), P(), P()),
        out_specs=(P(None, "row", "src"), P(None, None, ("row", "src"))),
        check_vma=False,
    )
```
